32 devices in a mesh: grp: 2 (over y), gx: 4 (over z), gy: 2 (over x), gz: 2 (over core).
Axes of the slice: x: 2, y: 2, z: 4, core: 2. Of those that a mesh axis runs over, the one named last changes fastest.
Arguments:
- ensemble: bfloat16 [128, 32, 32, 256], P(('grp', 'gx'), 'gy', 'gz'), parts along dimension 0, may hold values from -40 to 40
- wind_field: float32 [3, 128, 32, 32], P(None, ('grp', 'gx'), 'gy', 'gz'), parts along dimension 1, may hold values from -0.5 to 0.5
- obs_value: float32 [128, 32, 16], P(('grp', 'gx'), 'gy', 'gz'), parts along dimension 0, may hold values from -60 to 60
- obs_weight: float32 [128, 32, 16], P(('grp', 'gx'), 'gy', 'gz'), parts along dimension 0, may hold values from 0.1 to 1.75
- obs_cell: int32 [128, 32, 16], P(('grp', 'gx'), 'gy', 'gz'), parts along dimension 0, may hold values from 0 to 4095, as said below
- obs_used: int32 [128, 32, 16], P(('grp', 'gx'), 'gy', 'gz'), parts along dimension 0, may hold values 0 or 1
Outputs:
- analysis: bfloat16 [128, 32, 32, 256], P(('grp', 'gx'), 'gy', 'gz'), parts along dimension 0
The draws below stay inside these ranges and needn't reach their ends.
There are 2 independent parts, one for each index of `grp`. The reference program is written for one: setup_inputs(seed, part) draws one part's arguments, and reference() takes and returns one part's arrays. A program takes and returns all parts, laid end to end along the dimension named above; each array names one. Nothing has to cross between parts.
Inputs may be any that keep to these rules, and one draw needn't show every extreme that they name: `obs_cell`: each entry names a cell of the grid block held by the same device, numbered (x * 16 + y) * 16 + z inside the block.
All inputs are finite; a program needn't handle non-finite values. No bound on the sum of `obs_used` on one device may be relied on, other than what follows from the above.
Results may differ from the reference program's by a relative error of at most 0.0067.
Values may be sent and summed in bfloat16 or wider, within the bound.
A program may use at most 64 MiB of HBM per device.

```python
import math
import jax
import jax.numpy as jnp
from jax import lax

M = 256
CX = 16
CY = 16
CZ = 16
ITERS = 5
CELLS_FIRST = 64
CELLS_SECOND = 32
CELLS_THIRD = 32
OBS = 32768
N_GX = 4
N_GY = 2
N_GZ = 2


def member_spreads(key):
    key_scale = jax.random.fold_in(key, 202)
    return jnp.exp(jax.random.uniform(key_scale, (M,), jnp.float32, 0.0, 0.5 * math.log(10.0)))


def member_noise(key, index):
    key_member = jax.random.fold_in(jax.random.fold_in(key, 101), index)
    shape = (CELLS_FIRST, CELLS_SECOND, CELLS_THIRD)
    noise = jnp.clip(jax.random.normal(key_member, shape, jnp.float32), -4.0, 4.0)
    return noise


def prior_member(key, index):
    spreads = member_spreads(key)
    before = jnp.remainder(index + M - 1, M)
    return spreads[index] * (member_noise(key, index) + 0.6 * member_noise(key, before))


def draw_ensemble(key, part):
    members = jnp.arange(M, dtype=jnp.int32)
    stacked = jax.vmap(lambda index: prior_member(key, index))(members).astype(jnp.bfloat16)
    return jnp.moveaxis(stacked, 0, 3)


def observed_cells(key):
    shape = (CELLS_FIRST, CELLS_SECOND, CELLS_THIRD // 2)
    return jax.random.randint(jax.random.fold_in(key, 707), shape, 0, CX * CY * CZ, dtype=jnp.int32)


def draw_obs_cell(key, part):
    return observed_cells(key)


def draw_obs_value(key, part):
    shape = (CELLS_FIRST, CELLS_SECOND, CELLS_THIRD // 2)
    cells = observed_cells(key)
    chosen = jax.random.randint(jax.random.fold_in(key, 606), (), 0, M, dtype=jnp.int32)
    truth = prior_member(key, chosen)
    block_x = jnp.arange(CELLS_FIRST, dtype=jnp.int32)[:, None, None] // CX
    block_y = jnp.arange(CELLS_SECOND, dtype=jnp.int32)[None, :, None] // CY
    block_z = jnp.arange(CELLS_THIRD // 2, dtype=jnp.int32)[None, None, :] // (CZ // 2)
    place_x = block_x * CX + cells // (CY * CZ)
    place_y = block_y * CY + cells // CZ % CY
    place_z = block_z * CZ + cells % CZ
    error = jnp.clip(jax.random.normal(jax.random.fold_in(key, 808), shape, jnp.float32), -4.0, 4.0)
    return (2.0 * truth[place_x, place_y, place_z] + 0.5 * error).astype(jnp.float32)


def draw_obs_weight(key, part):
    key_main = jax.random.fold_in(key, 505)
    xpos = jnp.arange(CELLS_FIRST, dtype=jnp.float32)[:, None, None]
    rising = jnp.exp(xpos / (2.0 * (CELLS_FIRST - 1)) * math.log(3.0))
    shape = (CELLS_FIRST, CELLS_SECOND, CELLS_THIRD // 2)
    factor = jnp.exp(jax.random.uniform(key_main, shape, jnp.float32, math.log(0.1), 0.0))
    return (factor * rising).astype(jnp.float32)


def with_ends(array, own_key, low, largest):
    extent = array.shape
    spot = [jax.random.randint(jax.random.fold_in(own_key, axis), (), 0, extent[axis]) for axis in range(len(extent))]
    array = array.at[tuple(spot)].set(low)
    longest = extent.index(max(extent))
    spot[longest] = (spot[longest] + 1) % extent[longest]
    return array.at[tuple(spot)].set(largest)


def block_levels(own_key, extent, split, least, largest):
    def one(axis_at, blocks):
        draws = jax.random.uniform(jax.random.fold_in(jax.random.fold_in(own_key, 6), axis_at), (blocks,), jnp.float32, least / len(split), largest / len(split))
        return jnp.repeat(jnp.exp(draws), extent[axis_at] // blocks).reshape((-1,) + (1,) * (len(extent) - axis_at - 1))

    level = one(*split[0])
    for cut in split[1:]:
        level = level * one(*cut)
    return level


def setup_inputs(seed: int = 0, part: int = 0) -> dict:
    keys = jax.random.split(jax.random.key(seed), 7)
    part_keys = jax.random.split(jax.random.fold_in(keys[6], part), 7)
    ensemble = draw_ensemble(jax.random.fold_in(jax.random.fold_in(keys[6], part), 71), part)
    wind_field = jnp.clip(jax.random.uniform(part_keys[1], (3, CELLS_FIRST, CELLS_SECOND, CELLS_THIRD), jnp.float32, -0.5, 0.5) * block_levels(part_keys[1], (3, CELLS_FIRST, CELLS_SECOND, CELLS_THIRD), ((1, 4), (2, 2), (3, 2)), -0.4, 0.0), -0.5, 0.5)
    obs_value = draw_obs_value(jax.random.fold_in(jax.random.fold_in(keys[6], part), 71), part)
    obs_weight = draw_obs_weight(jax.random.fold_in(jax.random.fold_in(keys[6], part), 71), part)
    obs_cell = draw_obs_cell(jax.random.fold_in(jax.random.fold_in(keys[6], part), 71), part)
    obs_used = with_ends((jax.random.randint(part_keys[5], (CELLS_FIRST, CELLS_SECOND, CELLS_THIRD // 2), 0, 4) < 3).astype(jnp.int32), jax.random.fold_in(part_keys[5], 1), 0, 1)
    return {"ensemble": ensemble, "wind_field": wind_field, "obs_value": obs_value, "obs_weight": obs_weight, "obs_cell": obs_cell, "obs_used": obs_used}


diffusion = 0.1
steepen = 0.1
member_groups = 8

def advance(padded, wind_field):
    centre = padded[1:-1, 1:-1, 1:-1].astype(jnp.float32)
    ahead_x = padded[2:, 1:-1, 1:-1].astype(jnp.float32)
    behind_x = padded[:-2, 1:-1, 1:-1].astype(jnp.float32)
    ahead_y = padded[1:-1, 2:, 1:-1].astype(jnp.float32)
    behind_y = padded[1:-1, :-2, 1:-1].astype(jnp.float32)
    ahead_z = padded[1:-1, 1:-1, 2:].astype(jnp.float32)
    behind_z = padded[1:-1, 1:-1, :-2].astype(jnp.float32)
    laplace = ahead_x + behind_x + ahead_y + behind_y + ahead_z + behind_z - 6.0 * centre
    transport = (wind_field[0][..., None] + steepen * centre) * (ahead_x - behind_x)
    transport = transport + wind_field[1][..., None] * (ahead_y - behind_y)
    transport = transport + wind_field[2][..., None] * (ahead_z - behind_z)
    return lax.optimization_barrier((centre + diffusion * laplace - 0.5 * transport).astype(jnp.bfloat16))

def pad_cells(field):
    return jnp.pad(field, ((1, 1), (1, 1), (1, 1), (0, 0)))

def product(left, right):
    return jnp.dot(left, right, precision=lax.Precision.HIGHEST)

def inverse_root(gram_full):
    member_states = gram_full.shape[0]
    identity = jnp.eye(member_states, dtype=jnp.float32)
    coupled = identity + gram_full
    frob_norm = jnp.sqrt(jnp.sum(coupled * coupled))
    iterate_y = coupled / frob_norm
    iterate_z = identity
    for sweep in range(ITERS):
        factor_p = 0.5 * (3.0 * identity - product(iterate_z, iterate_y))
        iterate_y = product(factor_p, iterate_y)
        iterate_z = product(factor_p, iterate_z)
    return iterate_z / jnp.sqrt(frob_norm)

def to_blocks(field, depth):
    tail = field.shape[3:]
    shaped = field.reshape((N_GX, CX, N_GY, CY, N_GZ, depth) + tail)
    order = (0, 2, 4, 1, 3, 5) + tuple(range(6, 6 + len(tail)))
    return shaped.transpose(order).reshape((N_GX * N_GY * N_GZ, CX * CY * depth) + tail)

def reference(ensemble, wind_field, obs_value, obs_weight, obs_cell, obs_used):
    member_states = ensemble.shape[3]
    sorted_sets = ensemble.reshape(CELLS_FIRST, CELLS_SECOND, CELLS_THIRD, member_groups, member_states // member_groups).transpose(3, 0, 1, 2, 4)

    def predict_member_set(member_set):
        state = advance(pad_cells(member_set), wind_field)
        return advance(pad_cells(state), wind_field)
    predicted_state = lax.map(predict_member_set, sorted_sets).transpose(1, 2, 3, 0, 4).reshape(CELLS_FIRST, CELLS_SECOND, CELLS_THIRD, member_states)
    ensemble_average = lax.optimization_barrier(jnp.mean(predicted_state.astype(jnp.float32), axis=3))
    member_departures = lax.optimization_barrier((predicted_state.astype(jnp.float32) - ensemble_average[..., None]).astype(jnp.bfloat16))
    anom_blocks = to_blocks(member_departures, CZ)
    mean_blocks = to_blocks(ensemble_average, CZ)
    half_depth = CZ // 2
    cell_blocks = to_blocks(obs_cell, half_depth).astype(jnp.int32)
    picked = jnp.take_along_axis(anom_blocks, cell_blocks[..., None], axis=1).reshape(-1, member_states)
    mean_at = jnp.take_along_axis(mean_blocks, cell_blocks, axis=1).reshape(-1)
    in_use = to_blocks(obs_used, half_depth).reshape(-1).astype(jnp.float32)
    obs_scale = to_blocks(obs_weight, half_depth).reshape(-1)
    values = to_blocks(obs_value, half_depth).reshape(-1)
    scaled = ((in_use * obs_scale / math.sqrt(OBS))[:, None] * picked.astype(jnp.float32)).astype(jnp.bfloat16)
    scaled = lax.optimization_barrier(scaled)
    innovation = (in_use * obs_scale * (values - mean_at) / math.sqrt(OBS)).astype(jnp.bfloat16)
    innovation = lax.optimization_barrier(innovation)
    wide_scaled = scaled.astype(jnp.float32)
    gram_full = jnp.dot(wide_scaled.T, wide_scaled, precision=lax.Precision.HIGHEST)
    coupling = jnp.dot(innovation.astype(jnp.float32), wide_scaled, precision=lax.Precision.HIGHEST)
    transform = inverse_root(gram_full)
    shift = product(transform, product(transform, coupling))
    weights = lax.optimization_barrier((transform + shift[:, None]).astype(jnp.bfloat16))
    wide_weights = weights.astype(jnp.float32)
    flat_anom = member_departures.reshape(member_groups, -1, member_states)
    mean_flat = ensemble_average.reshape(member_groups, -1)

    def analyse(pair):
        block_anom, block_mean = pair
        mixed = jnp.dot(block_anom.astype(jnp.float32), wide_weights, precision=lax.Precision.HIGHEST)
        return (block_mean[:, None] + mixed).astype(jnp.bfloat16)
    analysis = lax.map(analyse, (flat_anom, mean_flat)).reshape(CELLS_FIRST, CELLS_SECOND, CELLS_THIRD, member_states)
    return analysis
```

```python
import functools

import jax
import jax.numpy as jnp
from jax import lax
from jax.experimental import pallas as pl
from jax.experimental.pallas import tpu as pltpu
from jax.sharding import PartitionSpec as P

ITERS = 5
DIFFUSION = 0.1
STEEPEN = 0.1
GRID_AXES = ("gx", "gy", "gz")
MESH = pl.DeviceIdType.MESH
F32 = jnp.float32
BF16 = jnp.bfloat16
VMEM = functools.partial(pl.BlockSpec, memory_space=pltpu.VMEM)
VMEM_LIMIT = 56 * 1024 * 1024


def product(left, right):
    return jnp.dot(left, right, precision=lax.Precision.HIGHEST, preferred_element_type=F32)


def contract(left, right, dims):
    return lax.dot_general(left, right, (dims, ((), ())), preferred_element_type=F32)


def collect_row(faces, y, piece, row):
    shift = (y % 8 - row) % 8
    moved = pltpu.roll(piece, shift, 0) if shift else piece
    rows = lax.broadcasted_iota(jnp.int32, piece.shape, 0)
    faces[y // 8] = moved if faces[y // 8] is None else jnp.where(rows == y % 8, moved, faces[y // 8])


def forecast_kernel(
    counts, ens, wind, spot_xz, spot_y, obs_sq, obs_sv,
    f_out, gram_out, coup_out,
    pad_a, pad_b, halo_z, in_x, in_y, in_z, out_x, out_y, out_z,
    obs_acc, root_w, pull_v, scaled, gram, send_sem, recv_sem,
):
    cx, cy, cz, members = ens.shape
    half = members // 2
    pos = [lax.axis_index(a) for a in GRID_AXES]
    has = [(pos[a] > 0, pos[a] < counts[a] - 1) for a in range(3)]
    inbox = (in_x, in_y, in_z)

    def target(a, d):
        where = pos[a] + (1 if d else counts[a] - 1)
        return {GRID_AXES[a]: lax.rem(where, counts[a])}

    def link(step, a, d):
        if a == 0:
            src = ens.at[(cx - 1) * d] if step == 0 else out_x.at[d]
        elif a == 1:
            src = ens.at[:, (cy - 1) * d] if step == 0 else out_y.at[d]
        else:
            src = out_z.at[step, d]
        return pltpu.make_async_remote_copy(
            src_ref=src,
            dst_ref=inbox[a].at[step, 1 - d],
            send_sem=send_sem.at[step, a, d],
            recv_sem=recv_sem.at[step, a, 1 - d],
            device_id=target(a, d),
            device_id_type=MESH,
        )

    def send(step, a):
        for d in range(2):
            @pl.when(has[a][d])
            def _():
                link(step, a, d).start()

    def receive(step, a, pad):
        for side in range(2):
            def border(values, a=a, side=side):
                if a == 0:
                    pad[(cx + 1) * side, 1 : cy + 1] = values
                elif a == 1:
                    pad[1 : cx + 1, (cy + 1) * side] = values
                else:
                    halo_z[side] = values

            @pl.when(has[a][side])
            def _():
                link(step, a, 1 - side).wait_recv()
                border(inbox[a][step, side].astype(F32))

            @pl.when(jnp.logical_not(has[a][side]))
            def _():
                border(jnp.zeros(inbox[a].shape[2:], F32))

    barrier = pltpu.get_barrier_semaphore()
    for a in range(3):
        for d in range(2):
            @pl.when(has[a][d])
            def _():
                pl.semaphore_signal(barrier, inc=1, device_id=target(a, d), device_id_type=MESH)
    neighbours = sum(has[a][d].astype(jnp.int32) for a in range(3) for d in range(2))
    pl.semaphore_wait(barrier, neighbours)

    send(0, 0)
    send(0, 1)

    def store_faces(step, x, first, last):
        out_z[step, 0, x] = jnp.concatenate(first, axis=0).astype(BF16)
        out_z[step, 1, x] = jnp.concatenate(last, axis=0).astype(BF16)

    def widen(x, carry):
        first, last = [None] * (cy // 8), [None] * (cy // 8)
        for y in range(cy):
            v = ens[x, y].astype(F32)
            pad_a[x + 1, y + 1] = v
            collect_row(first, y, v[:8], 0)
            collect_row(last, y, v[cz - 8 :], 7)
        store_faces(0, x, first, last)
        return carry

    lax.fori_loop(0, cx, widen, 0)
    send(0, 2)

    obs_acc[...] = jnp.zeros_like(obs_acc)
    chunks, chunk = spot_xz.shape

    def scatter(i, carry):
        row = pl.ds(i, 1)
        at_xz = lax.broadcasted_iota(jnp.int32, (cx * cz, chunk), 0) == spot_xz[row, :]
        at_y = lax.broadcasted_iota(jnp.int32, (cy, chunk), 0) == spot_y[row, :]
        parts = []
        for rest in (obs_sq[row, :], obs_sv[row, :]):
            for _ in range(3):
                part = rest.astype(BF16).astype(F32)
                parts.append(jnp.where(at_y, part, 0.0))
                rest = rest - part
        weighted = jnp.concatenate(parts, axis=0).astype(BF16)
        obs_acc[...] += contract(
            jnp.where(at_xz, 1.0, 0.0).astype(BF16), weighted, ((1,), (1,))
        )
        return carry

    lax.fori_loop(0, chunks, scatter, 0)
    sums = obs_acc[...]
    w_sum = sums[:, :cy] + sums[:, cy : 2 * cy] + sums[:, 2 * cy : 3 * cy]
    v_sum = sums[:, 3 * cy : 4 * cy] + sums[:, 4 * cy : 5 * cy] + sums[:, 5 * cy :]
    root_w[...] = jnp.sqrt(w_sum).reshape(cx, cz, cy)
    pull_v[...] = v_sum.reshape(cx, cz, cy)

    top = lax.broadcasted_iota(jnp.int32, (8, members), 0) == 0
    bottom = lax.broadcasted_iota(jnp.int32, (8, members), 0) == 7
    pieces = cz // 8

    def advance_row(pad, x, y):
        def rows(i, j):
            return [pad[i, j, 8 * k : 8 * k + 8] for k in range(pieces)]

        centre = rows(x + 1, y + 1)
        x_up, x_dn = rows(x + 2, y + 1), rows(x, y + 1)
        y_up, y_dn = rows(x + 1, y + 2), rows(x + 1, y)
        below = jnp.broadcast_to(halo_z[0, x, y : y + 1, :], (8, members))
        above = jnp.broadcast_to(halo_z[1, x, y : y + 1, :], (8, members))
        rolled_up = [pltpu.roll(c, 7, 0) for c in centre] + [above]
        rolled_dn = [below] + [pltpu.roll(c, 1, 0) for c in centre]
        result = []
        for k in range(pieces):
            c = centre[k]
            z_up = jnp.where(bottom, rolled_up[k + 1], rolled_up[k])
            z_dn = jnp.where(top, rolled_dn[k], rolled_dn[k + 1])
            wx, wy, wz = (wind[i, x, 8 * k : 8 * k + 8, y : y + 1] for i in range(3))
            laplace = ((x_up[k] + x_dn[k]) + (y_up[k] + y_dn[k])) + ((z_up + z_dn) - 6.0 * c)
            transport = (wx + (0.5 * STEEPEN) * c) * (x_up[k] - x_dn[k])
            transport = transport + wy * (y_up[k] - y_dn[k])
            transport = transport + wz * (z_up - z_dn)
            result.append(c + DIFFUSION * laplace - transport)
        return result

    for a in range(3):
        receive(0, a, pad_a)

    def first_step(x, carry):
        first, last = [None] * (cy // 8), [None] * (cy // 8)
        for y in range(cy):
            new = jnp.concatenate(advance_row(pad_a, x, y), axis=0).astype(BF16).astype(F32)
            pad_b[x + 1, y + 1] = new
            collect_row(first, y, new[:8], 0)
            collect_row(last, y, new[cz - 8 :], 7)
        store_faces(1, x, first, last)
        return carry

    lax.fori_loop(0, cx, first_step, 0)
    for d in range(2):
        out_x[d] = pad_b[1 + (cx - 1) * d, 1 : cy + 1].astype(BF16)
    send(1, 0)
    for d in range(2):
        out_y[d] = pad_b[1 : cx + 1, 1 + (cy - 1) * d].astype(BF16)
    send(1, 1)
    send(1, 2)
    for a in range(3):
        receive(1, a, pad_b)

    gram[...] = jnp.zeros_like(gram)
    ones = jnp.ones((members, half), BF16)

    def second_step(x, pulled):
        for y in range(cy):
            f_out[x, y] = jnp.concatenate(advance_row(pad_b, x, y), axis=0).astype(BF16)
        plane = f_out[x].reshape(cy * cz, members)
        mean = contract(plane, ones, ((1,), (0,))) * (1.0 / members)
        for y in range(cy):
            span = slice(y * cz, (y + 1) * cz)
            level = mean[span]
            root = jnp.broadcast_to(root_w[x, :, y : y + 1], (cz, half))
            pull = pull_v[x, :, y : y + 1] - root * root * level
            both = jnp.concatenate([level, level], axis=1)
            apart = (plane[span].astype(F32) - both).astype(BF16).astype(F32)
            scaled[span] = (apart * jnp.concatenate([root, root], axis=1)).astype(BF16)
            pulled = pulled + apart * jnp.concatenate([pull, pull], axis=1)
        block = scaled[...]
        gram[...] += contract(block, block, ((0,), (0,)))
        return pulled

    pulled = lax.fori_loop(0, cx, second_step, jnp.zeros((cz, members), F32))
    gram_out[:half] = gram[:half, :half]
    gram_out[half : 2 * half] = gram[:half, half:]
    gram_out[2 * half :] = gram[half:, half:]
    total = jnp.sum(pulled, axis=0, keepdims=True)
    coup_out[...] = jnp.concatenate(
        [total[:, :half], total[:, half:], jnp.zeros((6, half), F32)], axis=0
    )

    for step in range(2):
        for a in range(3):
            for d in range(2):
                @pl.when(has[a][d])
                def _():
                    link(step, a, d).wait_send()


def weights_from(tri, coup, half):
    members = 2 * half
    upper = tri[half : 2 * half]
    gram = jnp.concatenate(
        [
            jnp.concatenate([tri[:half], upper], axis=1),
            jnp.concatenate([upper.T, tri[2 * half :]], axis=1),
        ],
        axis=0,
    )
    shape = (members, members)
    diagonal = lax.broadcasted_iota(jnp.int32, shape, 0) == lax.broadcasted_iota(jnp.int32, shape, 1)
    identity = jnp.where(diagonal, 1.0, 0.0).astype(F32)
    coupled = identity + gram
    squares = jnp.sum(jnp.sum(coupled * coupled, axis=0, keepdims=True), axis=1, keepdims=True)
    norm = jnp.sqrt(squares)
    iterate_y = coupled / norm
    iterate_z = None
    for sweep in range(ITERS):
        inner = iterate_y if sweep == 0 else product(iterate_z, iterate_y)
        factor = 1.5 * identity - 0.5 * inner
        iterate_z = factor if sweep == 0 else product(factor, iterate_z)
        if sweep < ITERS - 1:
            iterate_y = product(factor, iterate_y)
    transform = iterate_z / jnp.sqrt(norm)
    coup_row = jnp.concatenate([coup[0:1], coup[1:2]], axis=1)
    coup_col = jnp.sum(jnp.where(diagonal, coup_row, 0.0), axis=1, keepdims=True)
    once_row = jnp.sum(transform * coup_col, axis=0, keepdims=True)
    shift = jnp.sum(transform * once_row, axis=1, keepdims=True)
    return (transform + shift).astype(BF16)


def reduce_kernel(counts, tri, coup, weights_out, outbox, inbox, own, full, semaphores):
    half = tri.shape[1]
    devices = counts[0] * counts[1] * counts[2]
    rows = tri.shape[0] // devices
    pos = [lax.axis_index(a) for a in GRID_AXES]
    rank = (pos[0] * counts[1] + pos[1]) * counts[2] + pos[2]

    def peer(k):
        return lax.rem(rank + k, devices)

    def device(r):
        return {
            "gx": r // (counts[1] * counts[2]),
            "gy": lax.rem(r // counts[2], counts[1]),
            "gz": lax.rem(r, counts[2]),
        }

    barrier = pltpu.get_barrier_semaphore()

    def each(action):
        def body(k, carry):
            action(k)
            return carry

        lax.fori_loop(1, devices, body, 0)

    each(lambda k: pl.semaphore_signal(barrier, inc=1, device_id=device(peer(k)), device_id_type=MESH))
    for i in range(devices):
        outbox[i, :rows] = tri[i * rows : (i + 1) * rows]
        outbox[i, rows:] = coup[...]
    pl.semaphore_wait(barrier, devices - 1)

    def scatter(to, origin):
        return pltpu.make_async_remote_copy(
            src_ref=outbox.at[to],
            dst_ref=inbox.at[origin],
            send_sem=semaphores.at[0, to],
            recv_sem=semaphores.at[1, origin],
            device_id=device(to),
            device_id_type=MESH,
        )

    def gather(to, origin):
        return pltpu.make_async_remote_copy(
            src_ref=own,
            dst_ref=full.at[origin],
            send_sem=semaphores.at[2, to],
            recv_sem=semaphores.at[3, origin],
            device_id=device(to),
            device_id_type=MESH,
        )

    each(lambda k: scatter(peer(k), rank).start())

    def add(k, total):
        scatter(peer(k), peer(k)).wait_recv()
        return total + inbox[peer(k)]

    total = lax.fori_loop(1, devices, add, outbox[rank])
    own[...] = total[:rows]
    full[rank] = total[:rows]
    each(lambda k: gather(peer(k), rank).start())
    each(lambda k: scatter(peer(k), rank).wait_send())
    each(lambda k: gather(peer(k), peer(k)).wait_recv())
    weights_out[...] = weights_from(full[...].reshape(3 * half, half), total[rows:], half)
    each(lambda k: gather(peer(k), rank).wait_send())


def analysis_kernel(f_ref, weights_ref, out_ref):
    shape = f_ref.shape
    members = shape[-1]
    plane = f_ref[...].reshape(-1, members)
    mean = contract(plane, jnp.ones((members, members), BF16), ((1,), (0,))) * (1.0 / members)
    apart = (plane.astype(F32) - mean).astype(BF16)
    mixed = contract(apart, weights_ref[...], ((1,), (0,)))
    out_ref[...] = (mean + mixed).astype(BF16).reshape(shape)


def weights_kernel(tri, coup, weights_out):
    weights_out[...] = weights_from(tri[...], coup[...], tri.shape[1])


def per_device(ensemble, wind_field, obs_value, obs_weight, obs_cell, obs_used):
    cx, cy, cz, members = ensemble.shape
    half = members // 2
    counts = tuple(lax.axis_size(a) for a in GRID_AXES)
    devices = counts[0] * counts[1] * counts[2]
    obs_total = obs_cell.size * devices

    chunked = (-1, 256)
    spot = obs_cell.reshape(chunked)
    spot_xz = spot // (cy * cz) * cz + spot % cz
    spot_y = spot // cz % cy
    strength = obs_used.astype(F32) * obs_weight
    obs_sq = (strength * strength / obs_total).reshape(chunked)
    obs_sv = obs_sq * obs_value.reshape(chunked)
    wind = 0.5 * wind_field.transpose(0, 1, 3, 2)

    forecast, tri, coup = pl.pallas_call(
        functools.partial(forecast_kernel, counts),
        out_shape=(
            jax.ShapeDtypeStruct(ensemble.shape, BF16),
            jax.ShapeDtypeStruct((3 * half, half), F32),
            jax.ShapeDtypeStruct((8, half), F32),
        ),
        in_specs=[VMEM()] * 6,
        out_specs=(VMEM(),) * 3,
        scratch_shapes=[
            pltpu.VMEM((cx + 2, cy + 2, cz, members), F32),
            pltpu.VMEM((cx + 2, cy + 2, cz, members), F32),
            pltpu.VMEM((2, cx, cy, members), F32),
            pltpu.VMEM((2, 2, cy, cz, members), BF16),
            pltpu.VMEM((2, 2, cx, cz, members), BF16),
            pltpu.VMEM((2, 2, cx, cy, members), BF16),
            pltpu.VMEM((2, cy, cz, members), BF16),
            pltpu.VMEM((2, cx, cz, members), BF16),
            pltpu.VMEM((2, 2, cx, cy, members), BF16),
            pltpu.VMEM((cx * cz, 6 * cy), F32),
            pltpu.VMEM((cx, cz, cy), F32),
            pltpu.VMEM((cx, cz, cy), F32),
            pltpu.VMEM((cy * cz, members), BF16),
            pltpu.VMEM((members, members), F32),
            pltpu.SemaphoreType.DMA((2, 3, 2)),
            pltpu.SemaphoreType.DMA((2, 3, 2)),
        ],
        compiler_params=pltpu.CompilerParams(
            collective_id=0, has_side_effects=True, vmem_limit_bytes=VMEM_LIMIT
        ),
    )(ensemble, wind, spot_xz, spot_y, obs_sq, obs_sv)

    weights_shape = jax.ShapeDtypeStruct((members, members), BF16)
    if devices > 1 and (3 * half // 8) % devices == 0:
        rows = 3 * half // devices
        weights = pl.pallas_call(
            functools.partial(reduce_kernel, counts),
            out_shape=weights_shape,
            in_specs=[VMEM()] * 2,
            out_specs=VMEM(),
            scratch_shapes=[
                pltpu.VMEM((devices, rows + 8, half), F32),
                pltpu.VMEM((devices, rows + 8, half), F32),
                pltpu.VMEM((rows, half), F32),
                pltpu.VMEM((devices, rows, half), F32),
                pltpu.SemaphoreType.DMA((4, devices)),
            ],
            compiler_params=pltpu.CompilerParams(
                collective_id=1, has_side_effects=True, vmem_limit_bytes=VMEM_LIMIT
            ),
        )(tri, coup)
    else:
        tri, coup = lax.psum((tri, coup), GRID_AXES)
        weights = pl.pallas_call(
            weights_kernel,
            out_shape=weights_shape,
            in_specs=[VMEM()] * 2,
            out_specs=VMEM(),
            compiler_params=pltpu.CompilerParams(vmem_limit_bytes=VMEM_LIMIT),
        )(tri, coup)

    planes = 4
    block = pl.BlockSpec((planes, cy, cz, members), lambda i: (i, 0, 0, 0))
    return pl.pallas_call(
        analysis_kernel,
        grid=(cx // planes,),
        out_shape=jax.ShapeDtypeStruct(ensemble.shape, BF16),
        in_specs=[block, pl.BlockSpec((members, members), lambda i: (0, 0))],
        out_specs=block,
        compiler_params=pltpu.CompilerParams(vmem_limit_bytes=VMEM_LIMIT),
    )(forecast, weights)


def solution(mesh):
    cells = P(("grp", "gx"), "gy", "gz")
    in_specs = (
        P(("grp", "gx"), "gy", "gz", None),
        P(None, ("grp", "gx"), "gy", "gz"),
        cells,
        cells,
        cells,
        cells,
    )
    out_specs = P(("grp", "gx"), "gy", "gz", None)
    return jax.shard_map(
        per_device, mesh=mesh, in_specs=in_specs, out_specs=out_specs, check_vma=False
    )
```

```python
import functools

import jax
import jax.numpy as jnp
from jax import lax
from jax.experimental import pallas as pl
from jax.experimental.pallas import tpu as pltpu
from jax.sharding import PartitionSpec as P

ITERS = 5
DIFFUSION = 0.1
STEEPEN = 0.1
GRID_AXES = ("gx", "gy", "gz")
MESH = pl.DeviceIdType.MESH
F32 = jnp.float32
BF16 = jnp.bfloat16
VMEM = functools.partial(pl.BlockSpec, memory_space=pltpu.VMEM)
VMEM_LIMIT = 56 * 1024 * 1024


def halves(value):
    high = value.astype(BF16)
    return high, (value - high.astype(F32)).astype(BF16)


def product(left, *rights):
    high, low = halves(left)
    wide = jnp.concatenate([high, high, low], axis=1)
    parts = [halves(right) for right in rights]
    tall = [jnp.concatenate([high, low, high], axis=0) for high, low in parts]
    return contract(wide, jnp.concatenate(tall, axis=1), ((1,), (0,)))


def contract(left, right, dims):
    return lax.dot_general(left, right, (dims, ((), ())), preferred_element_type=F32)


def collect_row(faces, y, piece, row):
    shift = (y % 8 - row) % 8
    moved = pltpu.roll(piece, shift, 0) if shift else piece
    rows = lax.broadcasted_iota(jnp.int32, piece.shape, 0)
    faces[y // 8] = moved if faces[y // 8] is None else jnp.where(rows == y % 8, moved, faces[y // 8])


def forecast_body(
    counts, enter, ens, wind, obs_value, obs_weight, obs_cell, obs_used,
    f_out, gram_out, coup_out,
    pad_a, pad_b, halo_z, in_x, in_y, in_z, out_x, out_y, out_z, wind_t,
    spot_xz, spot_y, obs_sq, obs_sv, obs_acc, root_w, pull_v, scaled, gram, send_sem, recv_sem,
):
    cx, cy, cz, members = ens.shape
    obs_total = obs_cell.size * counts[0] * counts[1] * counts[2]
    half = members // 2
    pos = [lax.axis_index(a) for a in GRID_AXES]
    has = [(pos[a] > 0, pos[a] < counts[a] - 1) for a in range(3)]
    inbox = (in_x, in_y, in_z)

    def target(a, d):
        where = pos[a] + (1 if d else counts[a] - 1)
        return {GRID_AXES[a]: lax.rem(where, counts[a])}

    def link(step, a, d):
        if a == 0:
            src = ens.at[(cx - 1) * d] if step == 0 else out_x.at[d]
        elif a == 1:
            src = ens.at[:, (cy - 1) * d] if step == 0 else out_y.at[d]
        else:
            src = out_z.at[step, d]
        return pltpu.make_async_remote_copy(
            src_ref=src,
            dst_ref=inbox[a].at[step, 1 - d],
            send_sem=send_sem.at[step, a, d],
            recv_sem=recv_sem.at[step, a, 1 - d],
            device_id=target(a, d),
            device_id_type=MESH,
        )

    def send(step, a):
        for d in range(2):
            @pl.when(has[a][d])
            def _():
                link(step, a, d).start()

    def receive(step, a, pad):
        for side in range(2):
            def border(values, a=a, side=side):
                if a == 0:
                    pad[(cx + 1) * side, 1 : cy + 1] = values
                elif a == 1:
                    pad[1 : cx + 1, (cy + 1) * side] = values
                else:
                    halo_z[side] = values

            @pl.when(has[a][side])
            def _():
                link(step, a, 1 - side).wait_recv()
                border(inbox[a][step, side].astype(F32))

            @pl.when(jnp.logical_not(has[a][side]))
            def _():
                border(jnp.zeros(inbox[a].shape[2:], F32))

    enter(has, target)
    send(0, 0)
    send(0, 1)

    def store_faces(step, x, first, last):
        out_z[step, 0, x] = jnp.concatenate(first, axis=0).astype(BF16)
        out_z[step, 1, x] = jnp.concatenate(last, axis=0).astype(BF16)

    def widen(x, carry):
        first, last = [None] * (cy // 8), [None] * (cy // 8)
        for y in range(cy):
            v = ens[x, y].astype(F32)
            pad_a[x + 1, y + 1] = v
            collect_row(first, y, v[:8], 0)
            collect_row(last, y, v[cz - 8 :], 7)
        store_faces(0, x, first, last)
        for i in range(3):
            wind_t[i, x] = 0.5 * wind[i, x].T
        return carry

    lax.fori_loop(0, cx, widen, 0)
    send(0, 2)

    obs_acc[...] = jnp.zeros_like(obs_acc)
    chunks, chunk = spot_xz.shape

    def turned(ref):
        return ref[...].reshape(chunk, chunks).T

    cell = turned(obs_cell)
    spot_xz[...] = cell // (cy * cz) * cz + cell % cz
    spot_y[...] = cell // cz % cy
    strength = turned(obs_used).astype(F32) * turned(obs_weight)
    squared = strength * strength * (1.0 / obs_total)
    obs_sq[...] = squared
    obs_sv[...] = squared * turned(obs_value)

    def scatter(i, carry):
        row = pl.ds(i, 1)
        at_xz = lax.broadcasted_iota(jnp.int32, (cx * cz, chunk), 0) == spot_xz[row, :]
        at_y = lax.broadcasted_iota(jnp.int32, (cy, chunk), 0) == spot_y[row, :]
        parts = []
        for rest in (obs_sq[row, :], obs_sv[row, :]):
            for _ in range(3):
                part = rest.astype(BF16).astype(F32)
                parts.append(jnp.where(at_y, part, 0.0))
                rest = rest - part
        weighted = jnp.concatenate(parts, axis=0).astype(BF16)
        obs_acc[...] += contract(
            jnp.where(at_xz, 1.0, 0.0).astype(BF16), weighted, ((1,), (1,))
        )
        return carry

    lax.fori_loop(0, chunks, scatter, 0)
    sums = obs_acc[...]
    w_sum = sums[:, :cy] + sums[:, cy : 2 * cy] + sums[:, 2 * cy : 3 * cy]
    v_sum = sums[:, 3 * cy : 4 * cy] + sums[:, 4 * cy : 5 * cy] + sums[:, 5 * cy :]
    root_w[...] = jnp.sqrt(w_sum).reshape(cx, cz, cy)
    pull_v[...] = v_sum.reshape(cx, cz, cy)

    top = lax.broadcasted_iota(jnp.int32, (8, members), 0) == 0
    bottom = lax.broadcasted_iota(jnp.int32, (8, members), 0) == 7
    pieces = cz // 8

    def advance_row(pad, x, y):
        def rows(i, j):
            return [pad[i, j, 8 * k : 8 * k + 8] for k in range(pieces)]

        centre = rows(x + 1, y + 1)
        x_up, x_dn = rows(x + 2, y + 1), rows(x, y + 1)
        y_up, y_dn = rows(x + 1, y + 2), rows(x + 1, y)
        below = jnp.broadcast_to(halo_z[0, x, y : y + 1, :], (8, members))
        above = jnp.broadcast_to(halo_z[1, x, y : y + 1, :], (8, members))
        rolled_up = [pltpu.roll(c, 7, 0) for c in centre] + [above]
        rolled_dn = [below] + [pltpu.roll(c, 1, 0) for c in centre]
        result = []
        for k in range(pieces):
            c = centre[k]
            z_up = jnp.where(bottom, rolled_up[k + 1], rolled_up[k])
            z_dn = jnp.where(top, rolled_dn[k], rolled_dn[k + 1])
            wx, wy, wz = (wind_t[i, x, 8 * k : 8 * k + 8, y : y + 1] for i in range(3))
            laplace = ((x_up[k] + x_dn[k]) + (y_up[k] + y_dn[k])) + ((z_up + z_dn) - 6.0 * c)
            transport = (wx + (0.5 * STEEPEN) * c) * (x_up[k] - x_dn[k])
            transport = transport + wy * (y_up[k] - y_dn[k])
            transport = transport + wz * (z_up - z_dn)
            result.append(c + DIFFUSION * laplace - transport)
        return result

    for a in range(3):
        receive(0, a, pad_a)

    def first_step(x, carry):
        first, last = [None] * (cy // 8), [None] * (cy // 8)
        for y in range(cy):
            new = jnp.concatenate(advance_row(pad_a, x, y), axis=0).astype(BF16).astype(F32)
            pad_b[x + 1, y + 1] = new
            collect_row(first, y, new[:8], 0)
            collect_row(last, y, new[cz - 8 :], 7)
        store_faces(1, x, first, last)
        return carry

    lax.fori_loop(0, cx, first_step, 0)
    for d in range(2):
        out_x[d] = pad_b[1 + (cx - 1) * d, 1 : cy + 1].astype(BF16)
    send(1, 0)
    for d in range(2):
        out_y[d] = pad_b[1 : cx + 1, 1 + (cy - 1) * d].astype(BF16)
    send(1, 1)
    send(1, 2)
    for a in range(3):
        receive(1, a, pad_b)

    gram[...] = jnp.zeros_like(gram)
    ones = jnp.ones((members, half), BF16)

    def second_step(x, pulled):
        for y in range(cy):
            f_out[x, y] = jnp.concatenate(advance_row(pad_b, x, y), axis=0).astype(BF16)
        plane = f_out[x].reshape(cy * cz, members)
        mean = contract(plane, ones, ((1,), (0,))) * (1.0 / members)
        for y in range(cy):
            span = slice(y * cz, (y + 1) * cz)
            level = mean[span]
            root = jnp.broadcast_to(root_w[x, :, y : y + 1], (cz, half))
            pull = pull_v[x, :, y : y + 1] - root * root * level
            both = jnp.concatenate([level, level], axis=1)
            apart = (plane[span].astype(F32) - both).astype(BF16).astype(F32)
            scaled[span] = (apart * jnp.concatenate([root, root], axis=1)).astype(BF16)
            pulled = pulled + apart * jnp.concatenate([pull, pull], axis=1)
        block = scaled[...]
        gram[...] += contract(block, block, ((0,), (0,)))
        return pulled

    pulled = lax.fori_loop(0, cx, second_step, jnp.zeros((cz, members), F32))
    gram_out[:half] = gram[:half, :half]
    gram_out[half : 2 * half] = gram[:half, half:]
    gram_out[2 * half :] = gram[half:, half:]
    total = jnp.sum(pulled, axis=0, keepdims=True)
    coup_out[...] = jnp.concatenate(
        [total[:, :half], total[:, half:], jnp.zeros((6, half), F32)], axis=0
    )

    def finish():
        for step in range(2):
            for a in range(3):
                for d in range(2):
                    @pl.when(has[a][d])
                    def _():
                        link(step, a, d).wait_send()

    return finish


def enter_beside(has, target):
    barrier = pltpu.get_barrier_semaphore()
    for a in range(3):
        for d in range(2):
            @pl.when(has[a][d])
            def _():
                pl.semaphore_signal(barrier, inc=1, device_id=target(a, d), device_id_type=MESH)
    neighbours = sum(has[a][d].astype(jnp.int32) for a in range(3) for d in range(2))
    pl.semaphore_wait(barrier, neighbours)


def forecast_kernel(counts, *refs):
    forecast_body(counts, enter_beside, *refs)()


def weights_from(tri, coup, half):
    members = 2 * half
    upper = tri[half : 2 * half]
    gram = jnp.concatenate(
        [
            jnp.concatenate([tri[:half], upper], axis=1),
            jnp.concatenate([upper.T, tri[2 * half :]], axis=1),
        ],
        axis=0,
    )
    shape = (members, members)
    diagonal = lax.broadcasted_iota(jnp.int32, shape, 0) == lax.broadcasted_iota(jnp.int32, shape, 1)
    identity = jnp.where(diagonal, 1.0, 0.0).astype(F32)
    coupled = identity + gram
    squares = jnp.sum(jnp.sum(coupled * coupled, axis=0, keepdims=True), axis=1, keepdims=True)
    norm = jnp.sqrt(squares)
    iterate_y = coupled / norm
    iterate_z = None
    for sweep in range(ITERS):
        inner = iterate_y if sweep == 0 else product(iterate_z, iterate_y)
        factor = 1.5 * identity - 0.5 * inner
        if sweep == 0:
            iterate_y, iterate_z = product(factor, iterate_y), factor
        elif sweep < ITERS - 1:
            both = product(factor, iterate_y, iterate_z)
            iterate_y, iterate_z = both[:, :members], both[:, members:]
        else:
            iterate_z = product(factor, iterate_z)
    transform = iterate_z / jnp.sqrt(norm)
    coup_row = jnp.concatenate([coup[0:1], coup[1:2]], axis=1)
    coup_col = jnp.sum(jnp.where(diagonal, coup_row, 0.0), axis=1, keepdims=True)
    once_row = jnp.sum(transform * coup_col, axis=0, keepdims=True)
    shift = jnp.sum(transform * once_row, axis=1, keepdims=True)
    weights = (transform + shift).astype(BF16).astype(F32)
    folded = weights + (1.0 - jnp.sum(weights, axis=0, keepdims=True)) / members
    return jnp.concatenate(halves(folded), axis=0)


def whole_kernel(counts, *refs):
    inputs, f_hbm, weights_out = refs[:6], refs[6], refs[7]
    outbox, inbox, own, full, semaphores, f_vmem, tri, coup, f_sem = refs[8:17]
    half = tri.shape[1]
    devices = counts[0] * counts[1] * counts[2]
    rows = tri.shape[0] // devices
    pos = [lax.axis_index(a) for a in GRID_AXES]
    rank = (pos[0] * counts[1] + pos[1]) * counts[2] + pos[2]

    def peer(k):
        return lax.rem(rank + k, devices)

    def device(r):
        return {
            "gx": r // (counts[1] * counts[2]),
            "gy": lax.rem(r // counts[2], counts[1]),
            "gz": lax.rem(r, counts[2]),
        }

    def each(action):
        def body(k, carry):
            action(k)
            return carry

        lax.fori_loop(1, devices, body, 0)

    def enter(has, target):
        barrier = pltpu.get_barrier_semaphore()
        each(
            lambda k: pl.semaphore_signal(
                barrier, inc=1, device_id=device(peer(k)), device_id_type=MESH
            )
        )
        pl.semaphore_wait(barrier, devices - 1)

    finish = forecast_body(counts, enter, *inputs, f_vmem, tri, coup, *refs[17:])
    write = pltpu.make_async_copy(f_vmem, f_hbm, f_sem)
    write.start()
    for i in range(devices):
        outbox[i, :rows] = tri[i * rows : (i + 1) * rows]
        outbox[i, rows:] = coup[...]

    def scatter(to, origin):
        return pltpu.make_async_remote_copy(
            src_ref=outbox.at[to],
            dst_ref=inbox.at[origin],
            send_sem=semaphores.at[0, to],
            recv_sem=semaphores.at[1, origin],
            device_id=device(to),
            device_id_type=MESH,
        )

    def gather(to, origin):
        return pltpu.make_async_remote_copy(
            src_ref=own,
            dst_ref=full.at[origin],
            send_sem=semaphores.at[2, to],
            recv_sem=semaphores.at[3, origin],
            device_id=device(to),
            device_id_type=MESH,
        )

    each(lambda k: scatter(peer(k), rank).start())

    def add(k, total):
        scatter(peer(k), peer(k)).wait_recv()
        return total + inbox[peer(k)]

    total = lax.fori_loop(1, devices, add, outbox[rank])
    own[...] = total[:rows]
    full[rank] = total[:rows]
    each(lambda k: gather(peer(k), rank).start())
    each(lambda k: scatter(peer(k), rank).wait_send())
    each(lambda k: gather(peer(k), peer(k)).wait_recv())
    weights_out[...] = weights_from(full[...].reshape(3 * half, half), total[rows:], half)
    each(lambda k: gather(peer(k), rank).wait_send())
    finish()
    write.wait()


def analysis_kernel(f_ref, folded_ref, out_ref):
    shape = f_ref.shape
    members = shape[-1]
    plane = f_ref[...].reshape(-1, members)
    twice = jnp.concatenate([plane, plane], axis=1)
    out_ref[...] = contract(twice, folded_ref[...], ((1,), (0,))).astype(BF16).reshape(shape)


def weights_kernel(tri, coup, weights_out):
    weights_out[...] = weights_from(tri[...], coup[...], tri.shape[1])


def per_device(ensemble, wind_field, obs_value, obs_weight, obs_cell, obs_used):
    cx, cy, cz, members = ensemble.shape
    half = members // 2
    counts = tuple(lax.axis_size(a) for a in GRID_AXES)
    devices = counts[0] * counts[1] * counts[2]
    chunk, chunks = cx * cy, obs_cell.shape[2]
    arguments = (ensemble, wind_field, obs_value, obs_weight, obs_cell, obs_used)
    forecast_shape = jax.ShapeDtypeStruct(ensemble.shape, BF16)
    folded_shape = jax.ShapeDtypeStruct((2 * members, members), BF16)
    tri_shape, coup_shape = (3 * half, half), (8, half)
    forecast_scratch = [
        pltpu.VMEM((cx + 2, cy + 2, cz, members), F32),
        pltpu.VMEM((cx + 2, cy + 2, cz, members), F32),
        pltpu.VMEM((2, cx, cy, members), F32),
        pltpu.VMEM((2, 2, cy, cz, members), BF16),
        pltpu.VMEM((2, 2, cx, cz, members), BF16),
        pltpu.VMEM((2, 2, cx, cy, members), BF16),
        pltpu.VMEM((2, cy, cz, members), BF16),
        pltpu.VMEM((2, cx, cz, members), BF16),
        pltpu.VMEM((2, 2, cx, cy, members), BF16),
        pltpu.VMEM((3, cx, cz, cy), F32),
        pltpu.VMEM((chunks, chunk), jnp.int32),
        pltpu.VMEM((chunks, chunk), jnp.int32),
        pltpu.VMEM((chunks, chunk), F32),
        pltpu.VMEM((chunks, chunk), F32),
        pltpu.VMEM((cx * cz, 6 * cy), F32),
        pltpu.VMEM((cx, cz, cy), F32),
        pltpu.VMEM((cx, cz, cy), F32),
        pltpu.VMEM((cy * cz, members), BF16),
        pltpu.VMEM((members, members), F32),
        pltpu.SemaphoreType.DMA((2, 3, 2)),
        pltpu.SemaphoreType.DMA((2, 3, 2)),
    ]
    if devices > 1 and (3 * half // 8) % devices == 0:
        rows = 3 * half // devices
        forecast, folded = pl.pallas_call(
            functools.partial(whole_kernel, counts),
            out_shape=(forecast_shape, folded_shape),
            in_specs=[VMEM()] * 6,
            out_specs=(pl.BlockSpec(memory_space=pl.ANY), VMEM()),
            scratch_shapes=[
                pltpu.VMEM((devices, rows + 8, half), F32),
                pltpu.VMEM((devices, rows + 8, half), F32),
                pltpu.VMEM((rows, half), F32),
                pltpu.VMEM((devices, rows, half), F32),
                pltpu.SemaphoreType.DMA((4, devices)),
                pltpu.VMEM(ensemble.shape, BF16),
                pltpu.VMEM(tri_shape, F32),
                pltpu.VMEM(coup_shape, F32),
                pltpu.SemaphoreType.DMA,
            ]
            + forecast_scratch,
            compiler_params=pltpu.CompilerParams(
                collective_id=0, has_side_effects=True, vmem_limit_bytes=VMEM_LIMIT
            ),
        )(*arguments)
    else:
        forecast, tri, coup = pl.pallas_call(
            functools.partial(forecast_kernel, counts),
            out_shape=(
                forecast_shape,
                jax.ShapeDtypeStruct(tri_shape, F32),
                jax.ShapeDtypeStruct(coup_shape, F32),
            ),
            in_specs=[VMEM()] * 6,
            out_specs=(VMEM(),) * 3,
            scratch_shapes=forecast_scratch,
            compiler_params=pltpu.CompilerParams(
                collective_id=0, has_side_effects=True, vmem_limit_bytes=VMEM_LIMIT
            ),
        )(*arguments)
        tri, coup = lax.psum((tri, coup), GRID_AXES)
        folded = pl.pallas_call(
            weights_kernel,
            out_shape=folded_shape,
            in_specs=[VMEM()] * 2,
            out_specs=VMEM(),
            compiler_params=pltpu.CompilerParams(vmem_limit_bytes=VMEM_LIMIT),
        )(tri, coup)

    planes = 4
    block = pl.BlockSpec((planes, cy, cz, members), lambda i: (i, 0, 0, 0))
    return pl.pallas_call(
        analysis_kernel,
        grid=(cx // planes,),
        out_shape=jax.ShapeDtypeStruct(ensemble.shape, BF16),
        in_specs=[block, pl.BlockSpec((2 * members, members), lambda i: (0, 0))],
        out_specs=block,
        compiler_params=pltpu.CompilerParams(vmem_limit_bytes=VMEM_LIMIT),
    )(forecast, folded)


def solution(mesh):
    cells = P(("grp", "gx"), "gy", "gz")
    in_specs = (
        P(("grp", "gx"), "gy", "gz", None),
        P(None, ("grp", "gx"), "gy", "gz"),
        cells,
        cells,
        cells,
        cells,
    )
    out_specs = P(("grp", "gx"), "gy", "gz", None)
    return jax.shard_map(
        per_device, mesh=mesh, in_specs=in_specs, out_specs=out_specs, check_vma=False
    )
```

```python
import functools

import jax
import jax.numpy as jnp
from jax import lax
from jax.experimental import pallas as pl
from jax.experimental.pallas import tpu as pltpu
from jax.sharding import PartitionSpec as P

ITERS = 5
DIFFUSION = 0.1
STEEPEN = 0.1
GRID_AXES = ("gx", "gy", "gz")
MESH = pl.DeviceIdType.MESH
F32 = jnp.float32
BF16 = jnp.bfloat16
VMEM = functools.partial(pl.BlockSpec, memory_space=pltpu.VMEM)
VMEM_LIMIT = 56 * 1024 * 1024


def halves(value):
    high = value.astype(BF16)
    return high, (value - high.astype(F32)).astype(BF16)


def product(left, *rights):
    high, low = halves(left)
    wide = jnp.concatenate([high, high, low], axis=1)
    parts = [halves(right) for right in rights]
    tall = [jnp.concatenate([high, low, high], axis=0) for high, low in parts]
    return contract(wide, jnp.concatenate(tall, axis=1), ((1,), (0,)))


def contract(left, right, dims):
    return lax.dot_general(left, right, (dims, ((), ())), preferred_element_type=F32)


def collect_row(faces, y, piece, row):
    shift = (y % 8 - row) % 8
    moved = pltpu.roll(piece, shift, 0) if shift else piece
    rows = lax.broadcasted_iota(jnp.int32, piece.shape, 0)
    faces[y // 8] = moved if faces[y // 8] is None else jnp.where(rows == y % 8, moved, faces[y // 8])


def forecast_body(
    counts, enter, ens, wind, obs_value, obs_weight, obs_cell, obs_used,
    f_out, gram_out, coup_out,
    pad_a, pad_b, halo_z, in_x, in_y, in_z, out_x, out_y, out_z, wind_t,
    spot_xz, spot_y, obs_sq, obs_sv, obs_acc, root_w, pull_v, scaled, gram, send_sem, recv_sem,
):
    cx, cy, cz, members = ens.shape
    obs_total = obs_cell.size * counts[0] * counts[1] * counts[2]
    half = members // 2
    pos = [lax.axis_index(a) for a in GRID_AXES]
    has = [(pos[a] > 0, pos[a] < counts[a] - 1) for a in range(3)]
    inbox = (in_x, in_y, in_z)

    def target(a, d):
        where = pos[a] + (1 if d else counts[a] - 1)
        return {GRID_AXES[a]: lax.rem(where, counts[a])}

    def link(step, a, d):
        if a == 0:
            src = ens.at[(cx - 1) * d] if step == 0 else out_x.at[d]
        elif a == 1:
            src = ens.at[:, (cy - 1) * d] if step == 0 else out_y.at[d]
        else:
            src = out_z.at[step, d]
        return pltpu.make_async_remote_copy(
            src_ref=src,
            dst_ref=inbox[a].at[step, 1 - d],
            send_sem=send_sem.at[step, a, d],
            recv_sem=recv_sem.at[step, a, 1 - d],
            device_id=target(a, d),
            device_id_type=MESH,
        )

    def send(step, a):
        for d in range(2):
            @pl.when(has[a][d])
            def _():
                link(step, a, d).start()

    def receive(step, a, pad):
        for side in range(2):
            def border(values, a=a, side=side):
                if a == 0:
                    pad[(cx + 1) * side, 1 : cy + 1] = values
                elif a == 1:
                    pad[1 : cx + 1, (cy + 1) * side] = values
                else:
                    halo_z[side] = values

            @pl.when(has[a][side])
            def _():
                link(step, a, 1 - side).wait_recv()
                border(inbox[a][step, side].astype(F32))

            @pl.when(jnp.logical_not(has[a][side]))
            def _():
                border(jnp.zeros(inbox[a].shape[2:], F32))

    enter(has, target)
    send(0, 0)
    send(0, 1)

    def store_faces(step, x, first, last):
        out_z[step, 0, x] = jnp.concatenate(first, axis=0).astype(BF16)
        out_z[step, 1, x] = jnp.concatenate(last, axis=0).astype(BF16)

    def widen(x, carry):
        first, last = [None] * (cy // 8), [None] * (cy // 8)
        for y in range(cy):
            v = ens[x, y].astype(F32)
            pad_a[x + 1, y + 1] = v
            collect_row(first, y, v[:8], 0)
            collect_row(last, y, v[cz - 8 :], 7)
        store_faces(0, x, first, last)
        for i in range(3):
            wind_t[i, x] = 0.5 * wind[i, x].T
        return carry

    lax.fori_loop(0, cx, widen, 0)
    send(0, 2)

    obs_acc[...] = jnp.zeros_like(obs_acc)
    chunks, chunk = spot_xz.shape

    def turned(ref):
        return ref[...].reshape(chunk, chunks).T

    cell = turned(obs_cell)
    spot_xz[...] = cell // (cy * cz) * cz + cell % cz
    spot_y[...] = cell // cz % cy
    strength = turned(obs_used).astype(F32) * turned(obs_weight)
    squared = strength * strength * (1.0 / obs_total)
    obs_sq[...] = squared
    obs_sv[...] = squared * turned(obs_value)

    def scatter(i, carry):
        row = pl.ds(i, 1)
        at_xz = lax.broadcasted_iota(jnp.int32, (cx * cz, chunk), 0) == spot_xz[row, :]
        at_y = lax.broadcasted_iota(jnp.int32, (cy, chunk), 0) == spot_y[row, :]
        parts = []
        for rest in (obs_sq[row, :], obs_sv[row, :]):
            for _ in range(3):
                part = rest.astype(BF16).astype(F32)
                parts.append(jnp.where(at_y, part, 0.0))
                rest = rest - part
        weighted = jnp.concatenate(parts, axis=0).astype(BF16)
        obs_acc[...] += contract(
            jnp.where(at_xz, 1.0, 0.0).astype(BF16), weighted, ((1,), (1,))
        )
        return carry

    lax.fori_loop(0, chunks, scatter, 0)
    sums = obs_acc[...]
    w_sum = sums[:, :cy] + sums[:, cy : 2 * cy] + sums[:, 2 * cy : 3 * cy]
    v_sum = sums[:, 3 * cy : 4 * cy] + sums[:, 4 * cy : 5 * cy] + sums[:, 5 * cy :]
    root_w[...] = jnp.sqrt(w_sum).reshape(cx, cz, cy)
    pull_v[...] = v_sum.reshape(cx, cz, cy)

    top = lax.broadcasted_iota(jnp.int32, (8, members), 0) == 0
    bottom = lax.broadcasted_iota(jnp.int32, (8, members), 0) == 7
    pieces = cz // 8

    def advance_row(pad, x, y):
        def rows(i, j):
            return [pad[i, j, 8 * k : 8 * k + 8] for k in range(pieces)]

        centre = rows(x + 1, y + 1)
        x_up, x_dn = rows(x + 2, y + 1), rows(x, y + 1)
        y_up, y_dn = rows(x + 1, y + 2), rows(x + 1, y)
        below = jnp.broadcast_to(halo_z[0, x, y : y + 1, :], (8, members))
        above = jnp.broadcast_to(halo_z[1, x, y : y + 1, :], (8, members))
        rolled_up = [pltpu.roll(c, 7, 0) for c in centre] + [above]
        rolled_dn = [below] + [pltpu.roll(c, 1, 0) for c in centre]
        result = []
        for k in range(pieces):
            c = centre[k]
            z_up = jnp.where(bottom, rolled_up[k + 1], rolled_up[k])
            z_dn = jnp.where(top, rolled_dn[k], rolled_dn[k + 1])
            wx, wy, wz = (wind_t[i, x, 8 * k : 8 * k + 8, y : y + 1] for i in range(3))
            laplace = ((x_up[k] + x_dn[k]) + (y_up[k] + y_dn[k])) + ((z_up + z_dn) - 6.0 * c)
            transport = (wx + (0.5 * STEEPEN) * c) * (x_up[k] - x_dn[k])
            transport = transport + wy * (y_up[k] - y_dn[k])
            transport = transport + wz * (z_up - z_dn)
            result.append(c + DIFFUSION * laplace - transport)
        return result

    for a in range(3):
        receive(0, a, pad_a)

    def first_step(x, carry):
        first, last = [None] * (cy // 8), [None] * (cy // 8)
        for y in range(cy):
            new = jnp.concatenate(advance_row(pad_a, x, y), axis=0).astype(BF16).astype(F32)
            pad_b[x + 1, y + 1] = new
            collect_row(first, y, new[:8], 0)
            collect_row(last, y, new[cz - 8 :], 7)
        store_faces(1, x, first, last)
        return carry

    lax.fori_loop(0, cx, first_step, 0)
    for d in range(2):
        out_x[d] = pad_b[1 + (cx - 1) * d, 1 : cy + 1].astype(BF16)
    send(1, 0)
    for d in range(2):
        out_y[d] = pad_b[1 : cx + 1, 1 + (cy - 1) * d].astype(BF16)
    send(1, 1)
    send(1, 2)
    for a in range(3):
        receive(1, a, pad_b)

    gram[...] = jnp.zeros_like(gram)
    ones = jnp.ones((members, half), BF16)

    def second_step(x, pulled):
        for y in range(cy):
            f_out[x, y] = jnp.concatenate(advance_row(pad_b, x, y), axis=0).astype(BF16)
        plane = f_out[x].reshape(cy * cz, members)
        mean = contract(plane, ones, ((1,), (0,))) * (1.0 / members)
        for y in range(cy):
            span = slice(y * cz, (y + 1) * cz)
            level = mean[span]
            root = jnp.broadcast_to(root_w[x, :, y : y + 1], (cz, half))
            pull = pull_v[x, :, y : y + 1] - root * root * level
            both = jnp.concatenate([level, level], axis=1)
            apart = (plane[span].astype(F32) - both).astype(BF16).astype(F32)
            scaled[span] = (apart * jnp.concatenate([root, root], axis=1)).astype(BF16)
            pulled = pulled + apart * jnp.concatenate([pull, pull], axis=1)
        block = scaled[...]
        gram[...] += contract(block, block, ((0,), (0,)))
        return pulled

    pulled = lax.fori_loop(0, cx, second_step, jnp.zeros((cz, members), F32))
    gram_out[:half] = gram[:half, :half]
    gram_out[half : 2 * half] = gram[:half, half:]
    gram_out[2 * half :] = gram[half:, half:]
    total = jnp.sum(pulled, axis=0, keepdims=True)
    coup_out[...] = jnp.concatenate(
        [total[:, :half], total[:, half:], jnp.zeros((6, half), F32)], axis=0
    )

    def finish():
        for step in range(2):
            for a in range(3):
                for d in range(2):
                    @pl.when(has[a][d])
                    def _():
                        link(step, a, d).wait_send()

    return finish


def enter_beside(has, target):
    barrier = pltpu.get_barrier_semaphore()
    for a in range(3):
        for d in range(2):
            @pl.when(has[a][d])
            def _():
                pl.semaphore_signal(barrier, inc=1, device_id=target(a, d), device_id_type=MESH)
    neighbours = sum(has[a][d].astype(jnp.int32) for a in range(3) for d in range(2))
    pl.semaphore_wait(barrier, neighbours)


def forecast_kernel(counts, *refs):
    forecast_body(counts, enter_beside, *refs)()


def weights_from(tri, coup, half):
    members = 2 * half
    upper = tri[half : 2 * half]
    gram = jnp.concatenate(
        [
            jnp.concatenate([tri[:half], upper], axis=1),
            jnp.concatenate([upper.T, tri[2 * half :]], axis=1),
        ],
        axis=0,
    )
    shape = (members, members)
    diagonal = lax.broadcasted_iota(jnp.int32, shape, 0) == lax.broadcasted_iota(jnp.int32, shape, 1)
    identity = jnp.where(diagonal, 1.0, 0.0).astype(F32)
    coupled = identity + gram
    squares = jnp.sum(jnp.sum(coupled * coupled, axis=0, keepdims=True), axis=1, keepdims=True)
    norm = jnp.sqrt(squares)
    iterate_y = coupled / norm
    iterate_z = None
    for sweep in range(ITERS):
        inner = iterate_y if sweep == 0 else product(iterate_z, iterate_y)
        factor = 1.5 * identity - 0.5 * inner
        if sweep == 0:
            iterate_y, iterate_z = product(factor, iterate_y), factor
        elif sweep < ITERS - 1:
            both = product(factor, iterate_y, iterate_z)
            iterate_y, iterate_z = both[:, :members], both[:, members:]
        else:
            iterate_z = product(factor, iterate_z)
    transform = iterate_z / jnp.sqrt(norm)
    coup_row = jnp.concatenate([coup[0:1], coup[1:2]], axis=1)
    coup_col = jnp.sum(jnp.where(diagonal, coup_row, 0.0), axis=1, keepdims=True)
    once_row = jnp.sum(transform * coup_col, axis=0, keepdims=True)
    shift = jnp.sum(transform * once_row, axis=1, keepdims=True)
    weights = (transform + shift).astype(BF16).astype(F32)
    folded = weights + (1.0 - jnp.sum(weights, axis=0, keepdims=True)) / members
    return jnp.concatenate(halves(folded), axis=0)


def whole_kernel(counts, *refs):
    inputs, f_hbm, weights_out = refs[:6], refs[6], refs[7]
    outbox, inbox, own, full, semaphores, f_vmem, tri, coup, f_sem = refs[8:17]
    half = tri.shape[1]
    devices = counts[0] * counts[1] * counts[2]
    rows = tri.shape[0] // devices
    pos = [lax.axis_index(a) for a in GRID_AXES]
    rank = (pos[0] * counts[1] + pos[1]) * counts[2] + pos[2]

    def peer(k):
        return lax.rem(rank + k, devices)

    def device(r):
        return {
            "gx": r // (counts[1] * counts[2]),
            "gy": lax.rem(r // counts[2], counts[1]),
            "gz": lax.rem(r, counts[2]),
        }

    def each(action):
        def body(k, carry):
            action(k)
            return carry

        lax.fori_loop(1, devices, body, 0)

    def enter(has, target):
        barrier = pltpu.get_barrier_semaphore()
        each(
            lambda k: pl.semaphore_signal(
                barrier, inc=1, device_id=device(peer(k)), device_id_type=MESH
            )
        )
        pl.semaphore_wait(barrier, devices - 1)

    finish = forecast_body(counts, enter, *inputs, f_vmem, tri, coup, *refs[17:])
    write = pltpu.make_async_copy(f_vmem, f_hbm, f_sem)
    write.start()
    for i in range(devices):
        outbox[i, :rows] = tri[i * rows : (i + 1) * rows]
        outbox[i, rows:] = coup[...]

    def scatter(to, origin):
        return pltpu.make_async_remote_copy(
            src_ref=outbox.at[to],
            dst_ref=inbox.at[origin],
            send_sem=semaphores.at[0, to],
            recv_sem=semaphores.at[1, origin],
            device_id=device(to),
            device_id_type=MESH,
        )

    def gather(to, origin):
        return pltpu.make_async_remote_copy(
            src_ref=own,
            dst_ref=full.at[origin],
            send_sem=semaphores.at[2, to],
            recv_sem=semaphores.at[3, origin],
            device_id=device(to),
            device_id_type=MESH,
        )

    each(lambda k: scatter(peer(k), rank).start())

    def add(k, total):
        scatter(peer(k), peer(k)).wait_recv()
        return total + inbox[peer(k)]

    total = lax.fori_loop(1, devices, add, outbox[rank])
    own[...] = total[:rows]
    full[rank] = total[:rows]
    each(lambda k: gather(peer(k), rank).start())
    each(lambda k: scatter(peer(k), rank).wait_send())
    each(lambda k: gather(peer(k), peer(k)).wait_recv())
    weights_out[...] = weights_from(full[...].reshape(3 * half, half), total[rows:], half)
    each(lambda k: gather(peer(k), rank).wait_send())
    finish()
    write.wait()


def analysis_kernel(f_ref, folded_ref, out_ref):
    shape = f_ref.shape
    members = shape[-1]
    plane = f_ref[...].reshape(-1, members)
    twice = jnp.concatenate([plane, plane], axis=1)
    out_ref[...] = contract(twice, folded_ref[...], ((1,), (0,))).astype(BF16).reshape(shape)


def weights_kernel(tri, coup, weights_out):
    weights_out[...] = weights_from(tri[...], coup[...], tri.shape[1])


def per_device(ensemble, wind_field, obs_value, obs_weight, obs_cell, obs_used):
    cx, cy, cz, members = ensemble.shape
    half = members // 2
    counts = tuple(lax.axis_size(a) for a in GRID_AXES)
    devices = counts[0] * counts[1] * counts[2]
    chunk, chunks = cx * obs_cell.shape[2], cy
    observed = (obs_value, obs_weight, obs_cell, obs_used)
    arguments = (ensemble, wind_field) + tuple(v.transpose(0, 2, 1) for v in observed)
    forecast_shape = jax.ShapeDtypeStruct(ensemble.shape, BF16)
    folded_shape = jax.ShapeDtypeStruct((2 * members, members), BF16)
    tri_shape, coup_shape = (3 * half, half), (8, half)
    forecast_scratch = [
        pltpu.VMEM((cx + 2, cy + 2, cz, members), F32),
        pltpu.VMEM((cx + 2, cy + 2, cz, members), F32),
        pltpu.VMEM((2, cx, cy, members), F32),
        pltpu.VMEM((2, 2, cy, cz, members), BF16),
        pltpu.VMEM((2, 2, cx, cz, members), BF16),
        pltpu.VMEM((2, 2, cx, cy, members), BF16),
        pltpu.VMEM((2, cy, cz, members), BF16),
        pltpu.VMEM((2, cx, cz, members), BF16),
        pltpu.VMEM((2, 2, cx, cy, members), BF16),
        pltpu.VMEM((3, cx, cz, cy), F32),
        pltpu.VMEM((chunks, chunk), jnp.int32),
        pltpu.VMEM((chunks, chunk), jnp.int32),
        pltpu.VMEM((chunks, chunk), F32),
        pltpu.VMEM((chunks, chunk), F32),
        pltpu.VMEM((cx * cz, 6 * cy), F32),
        pltpu.VMEM((cx, cz, cy), F32),
        pltpu.VMEM((cx, cz, cy), F32),
        pltpu.VMEM((cy * cz, members), BF16),
        pltpu.VMEM((members, members), F32),
        pltpu.SemaphoreType.DMA((2, 3, 2)),
        pltpu.SemaphoreType.DMA((2, 3, 2)),
    ]
    if devices > 1 and (3 * half // 8) % devices == 0:
        rows = 3 * half // devices
        forecast, folded = pl.pallas_call(
            functools.partial(whole_kernel, counts),
            out_shape=(forecast_shape, folded_shape),
            in_specs=[VMEM()] * 6,
            out_specs=(pl.BlockSpec(memory_space=pl.ANY), VMEM()),
            scratch_shapes=[
                pltpu.VMEM((devices, rows + 8, half), F32),
                pltpu.VMEM((devices, rows + 8, half), F32),
                pltpu.VMEM((rows, half), F32),
                pltpu.VMEM((devices, rows, half), F32),
                pltpu.SemaphoreType.DMA((4, devices)),
                pltpu.VMEM(ensemble.shape, BF16),
                pltpu.VMEM(tri_shape, F32),
                pltpu.VMEM(coup_shape, F32),
                pltpu.SemaphoreType.DMA,
            ]
            + forecast_scratch,
            compiler_params=pltpu.CompilerParams(
                collective_id=0, has_side_effects=True, vmem_limit_bytes=VMEM_LIMIT
            ),
        )(*arguments)
    else:
        forecast, tri, coup = pl.pallas_call(
            functools.partial(forecast_kernel, counts),
            out_shape=(
                forecast_shape,
                jax.ShapeDtypeStruct(tri_shape, F32),
                jax.ShapeDtypeStruct(coup_shape, F32),
            ),
            in_specs=[VMEM()] * 6,
            out_specs=(VMEM(),) * 3,
            scratch_shapes=forecast_scratch,
            compiler_params=pltpu.CompilerParams(
                collective_id=0, has_side_effects=True, vmem_limit_bytes=VMEM_LIMIT
            ),
        )(*arguments)
        tri, coup = lax.psum((tri, coup), GRID_AXES)
        folded = pl.pallas_call(
            weights_kernel,
            out_shape=folded_shape,
            in_specs=[VMEM()] * 2,
            out_specs=VMEM(),
            compiler_params=pltpu.CompilerParams(vmem_limit_bytes=VMEM_LIMIT),
        )(tri, coup)

    planes = 4
    block = pl.BlockSpec((planes, cy, cz, members), lambda i: (i, 0, 0, 0))
    return pl.pallas_call(
        analysis_kernel,
        grid=(cx // planes,),
        out_shape=jax.ShapeDtypeStruct(ensemble.shape, BF16),
        in_specs=[block, pl.BlockSpec((2 * members, members), lambda i: (0, 0))],
        out_specs=block,
        compiler_params=pltpu.CompilerParams(vmem_limit_bytes=VMEM_LIMIT),
    )(forecast, folded)


def solution(mesh):
    cells = P(("grp", "gx"), "gy", "gz")
    in_specs = (
        P(("grp", "gx"), "gy", "gz", None),
        P(None, ("grp", "gx"), "gy", "gz"),
        cells,
        cells,
        cells,
        cells,
    )
    out_specs = P(("grp", "gx"), "gy", "gz", None)
    return jax.shard_map(
        per_device, mesh=mesh, in_specs=in_specs, out_specs=out_specs, check_vma=False
    )
```

```python
import functools

import jax
import jax.numpy as jnp
from jax import lax
from jax.experimental import pallas as pl
from jax.experimental.pallas import tpu as pltpu
from jax.sharding import PartitionSpec as P

ITERS = 5
DIFFUSION = 0.1
STEEPEN = 0.1
GRID_AXES = ("gx", "gy", "gz")
MESH = pl.DeviceIdType.MESH
F32 = jnp.float32
BF16 = jnp.bfloat16
VMEM = functools.partial(pl.BlockSpec, memory_space=pltpu.VMEM)
VMEM_LIMIT = 56 * 1024 * 1024


def halves(value):
    high = value.astype(BF16)
    return high, (value - high.astype(F32)).astype(BF16)


def product(left, *rights):
    high, low = halves(left)
    wide = jnp.concatenate([high, high, low], axis=1)
    parts = [halves(right) for right in rights]
    tall = [jnp.concatenate([high, low, high], axis=0) for high, low in parts]
    return contract(wide, jnp.concatenate(tall, axis=1), ((1,), (0,)))


def contract(left, right, dims):
    return lax.dot_general(left, right, (dims, ((), ())), preferred_element_type=F32)


def collect_row(faces, y, piece, row):
    shift = (y % 8 - row) % 8
    moved = pltpu.roll(piece, shift, 0) if shift else piece
    rows = lax.broadcasted_iota(jnp.int32, piece.shape, 0)
    faces[y // 8] = moved if faces[y // 8] is None else jnp.where(rows == y % 8, moved, faces[y // 8])


def forecast_body(
    counts, enter, ens, wind, obs_value, obs_weight, obs_cell, obs_used,
    f_out, gram_out, coup_out,
    pad_a, pad_b, halo_z, in_x, in_y, in_z, out_x, out_y, out_z, wind_t,
    spot_xz, spot_y, obs_sq, obs_sv, obs_acc, root_w, pull_v, scaled, gram, send_sem, recv_sem,
):
    cx, cy, cz, members = ens.shape
    obs_total = obs_cell.size * counts[0] * counts[1] * counts[2]
    half = members // 2
    pos = [lax.axis_index(a) for a in GRID_AXES]
    has = [(pos[a] > 0, pos[a] < counts[a] - 1) for a in range(3)]
    inbox = (in_x, in_y, in_z)

    def target(a, d):
        where = pos[a] + (1 if d else counts[a] - 1)
        return {GRID_AXES[a]: lax.rem(where, counts[a])}

    def link(step, a, d):
        if a == 0:
            src = ens.at[(cx - 1) * d] if step == 0 else out_x.at[d]
        elif a == 1:
            src = ens.at[:, (cy - 1) * d] if step == 0 else out_y.at[d]
        else:
            src = out_z.at[step, d]
        return pltpu.make_async_remote_copy(
            src_ref=src,
            dst_ref=inbox[a].at[step, 1 - d],
            send_sem=send_sem.at[step, a, d],
            recv_sem=recv_sem.at[step, a, 1 - d],
            device_id=target(a, d),
            device_id_type=MESH,
        )

    def send(step, a):
        for d in range(2):
            @pl.when(has[a][d])
            def _():
                link(step, a, d).start()

    def receive(step, a, pad):
        for side in range(2):
            def border(values, a=a, side=side):
                if a == 0:
                    pad[(cx + 1) * side, 1 : cy + 1] = values
                elif a == 1:
                    pad[1 : cx + 1, (cy + 1) * side] = values
                else:
                    halo_z[side] = values

            @pl.when(has[a][side])
            def _():
                link(step, a, 1 - side).wait_recv()
                border(inbox[a][step, side].astype(F32))

            @pl.when(jnp.logical_not(has[a][side]))
            def _():
                border(jnp.zeros(inbox[a].shape[2:], F32))

    enter(has, target)
    send(0, 0)
    send(0, 1)

    def store_faces(step, x, first, last):
        out_z[step, 0, x] = jnp.concatenate(first, axis=0).astype(BF16)
        out_z[step, 1, x] = jnp.concatenate(last, axis=0).astype(BF16)

    def widen(x, carry):
        first, last = [None] * (cy // 8), [None] * (cy // 8)
        for y in range(cy):
            v = ens[x, y].astype(F32)
            pad_a[x + 1, y + 1] = v
            collect_row(first, y, v[:8], 0)
            collect_row(last, y, v[cz - 8 :], 7)
        store_faces(0, x, first, last)
        for i in range(3):
            wind_t[i, x] = 0.5 * wind[i, x].T
        return carry

    lax.fori_loop(0, cx, widen, 0)
    send(0, 2)

    obs_acc[...] = jnp.zeros_like(obs_acc)
    chunks, chunk = spot_xz.shape

    def turned(ref):
        return ref[...].reshape(chunk, chunks).T

    cell = turned(obs_cell)
    spot_xz[...] = cell // (cy * cz) * cz + cell % cz
    spot_y[...] = cell // cz % cy
    strength = turned(obs_used).astype(F32) * turned(obs_weight)
    squared = strength * strength * (1.0 / obs_total)
    obs_sq[...] = squared
    obs_sv[...] = squared * turned(obs_value)

    def scatter(i, carry):
        row = pl.ds(i, 1)
        at_xz = lax.broadcasted_iota(jnp.int32, (cx * cz, chunk), 0) == spot_xz[row, :]
        at_y = lax.broadcasted_iota(jnp.int32, (cy, chunk), 0) == spot_y[row, :]
        parts = []
        for rest in (obs_sq[row, :], obs_sv[row, :]):
            for _ in range(3):
                part = rest.astype(BF16).astype(F32)
                parts.append(jnp.where(at_y, part, 0.0))
                rest = rest - part
        weighted = jnp.concatenate(parts, axis=0).astype(BF16)
        obs_acc[...] += contract(
            jnp.where(at_xz, 1.0, 0.0).astype(BF16), weighted, ((1,), (1,))
        )
        return carry

    lax.fori_loop(0, chunks, scatter, 0)
    sums = obs_acc[...]
    w_sum = sums[:, :cy] + sums[:, cy : 2 * cy] + sums[:, 2 * cy : 3 * cy]
    v_sum = sums[:, 3 * cy : 4 * cy] + sums[:, 4 * cy : 5 * cy] + sums[:, 5 * cy :]
    root_w[...] = jnp.sqrt(w_sum).reshape(cx, cz, cy)
    pull_v[...] = v_sum.reshape(cx, cz, cy)

    top = lax.broadcasted_iota(jnp.int32, (8, members), 0) == 0
    bottom = lax.broadcasted_iota(jnp.int32, (8, members), 0) == 7
    pieces = cz // 8

    def advance_row(pad, x, y):
        def rows(i, j):
            return [pad[i, j, 8 * k : 8 * k + 8] for k in range(pieces)]

        centre = rows(x + 1, y + 1)
        x_up, x_dn = rows(x + 2, y + 1), rows(x, y + 1)
        y_up, y_dn = rows(x + 1, y + 2), rows(x + 1, y)
        below = jnp.broadcast_to(halo_z[0, x, y : y + 1, :], (8, members))
        above = jnp.broadcast_to(halo_z[1, x, y : y + 1, :], (8, members))
        rolled_up = [pltpu.roll(c, 7, 0) for c in centre] + [above]
        rolled_dn = [below] + [pltpu.roll(c, 1, 0) for c in centre]
        result = []
        for k in range(pieces):
            c = centre[k]
            z_up = jnp.where(bottom, rolled_up[k + 1], rolled_up[k])
            z_dn = jnp.where(top, rolled_dn[k], rolled_dn[k + 1])
            wx, wy, wz = (wind_t[i, x, 8 * k : 8 * k + 8, y : y + 1] for i in range(3))
            laplace = ((x_up[k] + x_dn[k]) + (y_up[k] + y_dn[k])) + ((z_up + z_dn) - 6.0 * c)
            transport = (wx + (0.5 * STEEPEN) * c) * (x_up[k] - x_dn[k])
            transport = transport + wy * (y_up[k] - y_dn[k])
            transport = transport + wz * (z_up - z_dn)
            result.append(c + DIFFUSION * laplace - transport)
        return result

    for a in range(3):
        receive(0, a, pad_a)

    def first_step(x, carry):
        first, last = [None] * (cy // 8), [None] * (cy // 8)
        for y in range(cy):
            new = jnp.concatenate(advance_row(pad_a, x, y), axis=0).astype(BF16).astype(F32)
            pad_b[x + 1, y + 1] = new
            collect_row(first, y, new[:8], 0)
            collect_row(last, y, new[cz - 8 :], 7)
        store_faces(1, x, first, last)
        return carry

    lax.fori_loop(0, 2, lambda i, carry: first_step(i * (cx - 1), carry), 0)
    for d in range(2):
        out_x[d] = pad_b[1 + (cx - 1) * d, 1 : cy + 1].astype(BF16)
    send(1, 0)
    lax.fori_loop(1, cx - 1, first_step, 0)
    for d in range(2):
        out_y[d] = pad_b[1 : cx + 1, 1 + (cy - 1) * d].astype(BF16)
    send(1, 1)
    send(1, 2)
    for a in range(3):
        receive(1, a, pad_b)

    gram[...] = jnp.zeros_like(gram)
    ones = jnp.ones((members, half), BF16)

    def second_step(x, pulled):
        for y in range(cy):
            f_out[x, y] = jnp.concatenate(advance_row(pad_b, x, y), axis=0).astype(BF16)
        plane = f_out[x].reshape(cy * cz, members)
        mean = contract(plane, ones, ((1,), (0,))) * (1.0 / members)
        for y in range(cy):
            span = slice(y * cz, (y + 1) * cz)
            level = mean[span]
            root = jnp.broadcast_to(root_w[x, :, y : y + 1], (cz, half))
            pull = pull_v[x, :, y : y + 1] - root * root * level
            both = jnp.concatenate([level, level], axis=1)
            apart = (plane[span].astype(F32) - both).astype(BF16).astype(F32)
            scaled[span] = (apart * jnp.concatenate([root, root], axis=1)).astype(BF16)
            pulled = pulled + apart * jnp.concatenate([pull, pull], axis=1)
        block = scaled[...]
        gram[...] += contract(block, block, ((0,), (0,)))
        return pulled

    pulled = lax.fori_loop(0, cx, second_step, jnp.zeros((cz, members), F32))
    gram_out[:half] = gram[:half, :half]
    gram_out[half : 2 * half] = gram[:half, half:]
    gram_out[2 * half :] = gram[half:, half:]
    total = jnp.sum(pulled, axis=0, keepdims=True)
    coup_out[...] = jnp.concatenate(
        [total[:, :half], total[:, half:], jnp.zeros((6, half), F32)], axis=0
    )

    def finish():
        for step in range(2):
            for a in range(3):
                for d in range(2):
                    @pl.when(has[a][d])
                    def _():
                        link(step, a, d).wait_send()

    return finish


def enter_beside(has, target):
    barrier = pltpu.get_barrier_semaphore()
    for a in range(3):
        for d in range(2):
            @pl.when(has[a][d])
            def _():
                pl.semaphore_signal(barrier, inc=1, device_id=target(a, d), device_id_type=MESH)
    neighbours = sum(has[a][d].astype(jnp.int32) for a in range(3) for d in range(2))
    pl.semaphore_wait(barrier, neighbours)


def forecast_kernel(counts, *refs):
    forecast_body(counts, enter_beside, *refs)()


def weights_from(tri, coup, half):
    members = 2 * half
    upper = tri[half : 2 * half]
    gram = jnp.concatenate(
        [
            jnp.concatenate([tri[:half], upper], axis=1),
            jnp.concatenate([upper.T, tri[2 * half :]], axis=1),
        ],
        axis=0,
    )
    shape = (members, members)
    diagonal = lax.broadcasted_iota(jnp.int32, shape, 0) == lax.broadcasted_iota(jnp.int32, shape, 1)
    identity = jnp.where(diagonal, 1.0, 0.0).astype(F32)
    coupled = identity + gram
    squares = jnp.sum(jnp.sum(coupled * coupled, axis=0, keepdims=True), axis=1, keepdims=True)
    norm = jnp.sqrt(squares)
    iterate_y = coupled / norm
    iterate_z = None
    for sweep in range(ITERS):
        inner = iterate_y if sweep == 0 else product(iterate_z, iterate_y)
        factor = 1.5 * identity - 0.5 * inner
        if sweep == 0:
            iterate_y, iterate_z = product(factor, iterate_y), factor
        elif sweep < ITERS - 1:
            both = product(factor, iterate_y, iterate_z)
            iterate_y, iterate_z = both[:, :members], both[:, members:]
        else:
            iterate_z = product(factor, iterate_z)
    transform = iterate_z / jnp.sqrt(norm)
    coup_row = jnp.concatenate([coup[0:1], coup[1:2]], axis=1)
    coup_col = jnp.sum(jnp.where(diagonal, coup_row, 0.0), axis=1, keepdims=True)
    once_row = jnp.sum(transform * coup_col, axis=0, keepdims=True)
    shift = jnp.sum(transform * once_row, axis=1, keepdims=True)
    weights = (transform + shift).astype(BF16).astype(F32)
    folded = weights + (1.0 - jnp.sum(weights, axis=0, keepdims=True)) / members
    return jnp.concatenate(halves(folded), axis=0)


def whole_kernel(counts, *refs):
    inputs, f_hbm, weights_out = refs[:6], refs[6], refs[7]
    outbox, inbox, own, full, semaphores, f_vmem, tri, coup, f_sem = refs[8:17]
    half = tri.shape[1]
    devices = counts[0] * counts[1] * counts[2]
    rows = tri.shape[0] // devices
    pos = [lax.axis_index(a) for a in GRID_AXES]
    rank = (pos[0] * counts[1] + pos[1]) * counts[2] + pos[2]

    def peer(k):
        return lax.rem(rank + k, devices)

    def device(r):
        return {
            "gx": r // (counts[1] * counts[2]),
            "gy": lax.rem(r // counts[2], counts[1]),
            "gz": lax.rem(r, counts[2]),
        }

    def each(action):
        def body(k, carry):
            action(k)
            return carry

        lax.fori_loop(1, devices, body, 0)

    def enter(has, target):
        barrier = pltpu.get_barrier_semaphore()
        each(
            lambda k: pl.semaphore_signal(
                barrier, inc=1, device_id=device(peer(k)), device_id_type=MESH
            )
        )
        pl.semaphore_wait(barrier, devices - 1)

    finish = forecast_body(counts, enter, *inputs, f_vmem, tri, coup, *refs[17:])
    write = pltpu.make_async_copy(f_vmem, f_hbm, f_sem)
    write.start()
    for i in range(devices):
        outbox[i, :rows] = tri[i * rows : (i + 1) * rows]
        outbox[i, rows:] = coup[...]

    def scatter(to, origin):
        return pltpu.make_async_remote_copy(
            src_ref=outbox.at[to],
            dst_ref=inbox.at[origin],
            send_sem=semaphores.at[0, to],
            recv_sem=semaphores.at[1, origin],
            device_id=device(to),
            device_id_type=MESH,
        )

    def gather(to, origin):
        return pltpu.make_async_remote_copy(
            src_ref=own,
            dst_ref=full.at[origin],
            send_sem=semaphores.at[2, to],
            recv_sem=semaphores.at[3, origin],
            device_id=device(to),
            device_id_type=MESH,
        )

    each(lambda k: scatter(peer(k), rank).start())

    def add(k, total):
        scatter(peer(k), peer(k)).wait_recv()
        return total + inbox[peer(k)]

    total = lax.fori_loop(1, devices, add, outbox[rank])
    own[...] = total[:rows]
    full[rank] = total[:rows]
    each(lambda k: gather(peer(k), rank).start())
    each(lambda k: scatter(peer(k), rank).wait_send())
    each(lambda k: gather(peer(k), peer(k)).wait_recv())
    weights_out[...] = weights_from(full[...].reshape(3 * half, half), total[rows:], half)
    each(lambda k: gather(peer(k), rank).wait_send())
    finish()
    write.wait()


def analysis_kernel(f_ref, folded_ref, out_ref):
    shape = f_ref.shape
    members = shape[-1]
    plane = f_ref[...].reshape(-1, members)
    twice = jnp.concatenate([plane, plane], axis=1)
    out_ref[...] = contract(twice, folded_ref[...], ((1,), (0,))).astype(BF16).reshape(shape)


def weights_kernel(tri, coup, weights_out):
    weights_out[...] = weights_from(tri[...], coup[...], tri.shape[1])


def per_device(ensemble, wind_field, obs_value, obs_weight, obs_cell, obs_used):
    cx, cy, cz, members = ensemble.shape
    half = members // 2
    counts = tuple(lax.axis_size(a) for a in GRID_AXES)
    devices = counts[0] * counts[1] * counts[2]
    chunk, chunks = cx * obs_cell.shape[2], cy
    observed = (obs_value, obs_weight, obs_cell, obs_used)
    arguments = (ensemble, wind_field) + tuple(v.transpose(0, 2, 1) for v in observed)
    forecast_shape = jax.ShapeDtypeStruct(ensemble.shape, BF16)
    folded_shape = jax.ShapeDtypeStruct((2 * members, members), BF16)
    tri_shape, coup_shape = (3 * half, half), (8, half)
    forecast_scratch = [
        pltpu.VMEM((cx + 2, cy + 2, cz, members), F32),
        pltpu.VMEM((cx + 2, cy + 2, cz, members), F32),
        pltpu.VMEM((2, cx, cy, members), F32),
        pltpu.VMEM((2, 2, cy, cz, members), BF16),
        pltpu.VMEM((2, 2, cx, cz, members), BF16),
        pltpu.VMEM((2, 2, cx, cy, members), BF16),
        pltpu.VMEM((2, cy, cz, members), BF16),
        pltpu.VMEM((2, cx, cz, members), BF16),
        pltpu.VMEM((2, 2, cx, cy, members), BF16),
        pltpu.VMEM((3, cx, cz, cy), F32),
        pltpu.VMEM((chunks, chunk), jnp.int32),
        pltpu.VMEM((chunks, chunk), jnp.int32),
        pltpu.VMEM((chunks, chunk), F32),
        pltpu.VMEM((chunks, chunk), F32),
        pltpu.VMEM((cx * cz, 6 * cy), F32),
        pltpu.VMEM((cx, cz, cy), F32),
        pltpu.VMEM((cx, cz, cy), F32),
        pltpu.VMEM((cy * cz, members), BF16),
        pltpu.VMEM((members, members), F32),
        pltpu.SemaphoreType.DMA((2, 3, 2)),
        pltpu.SemaphoreType.DMA((2, 3, 2)),
    ]
    if devices > 1 and (3 * half // 8) % devices == 0:
        rows = 3 * half // devices
        forecast, folded = pl.pallas_call(
            functools.partial(whole_kernel, counts),
            out_shape=(forecast_shape, folded_shape),
            in_specs=[VMEM()] * 6,
            out_specs=(pl.BlockSpec(memory_space=pl.ANY), VMEM()),
            scratch_shapes=[
                pltpu.VMEM((devices, rows + 8, half), F32),
                pltpu.VMEM((devices, rows + 8, half), F32),
                pltpu.VMEM((rows, half), F32),
                pltpu.VMEM((devices, rows, half), F32),
                pltpu.SemaphoreType.DMA((4, devices)),
                pltpu.VMEM(ensemble.shape, BF16),
                pltpu.VMEM(tri_shape, F32),
                pltpu.VMEM(coup_shape, F32),
                pltpu.SemaphoreType.DMA,
            ]
            + forecast_scratch,
            compiler_params=pltpu.CompilerParams(
                collective_id=0, has_side_effects=True, vmem_limit_bytes=VMEM_LIMIT
            ),
        )(*arguments)
    else:
        forecast, tri, coup = pl.pallas_call(
            functools.partial(forecast_kernel, counts),
            out_shape=(
                forecast_shape,
                jax.ShapeDtypeStruct(tri_shape, F32),
                jax.ShapeDtypeStruct(coup_shape, F32),
            ),
            in_specs=[VMEM()] * 6,
            out_specs=(VMEM(),) * 3,
            scratch_shapes=forecast_scratch,
            compiler_params=pltpu.CompilerParams(
                collective_id=0, has_side_effects=True, vmem_limit_bytes=VMEM_LIMIT
            ),
        )(*arguments)
        tri, coup = lax.psum((tri, coup), GRID_AXES)
        folded = pl.pallas_call(
            weights_kernel,
            out_shape=folded_shape,
            in_specs=[VMEM()] * 2,
            out_specs=VMEM(),
            compiler_params=pltpu.CompilerParams(vmem_limit_bytes=VMEM_LIMIT),
        )(tri, coup)

    planes = 8
    block = pl.BlockSpec((planes, cy, cz, members), lambda i: (i, 0, 0, 0))
    return pl.pallas_call(
        analysis_kernel,
        grid=(cx // planes,),
        out_shape=jax.ShapeDtypeStruct(ensemble.shape, BF16),
        in_specs=[block, pl.BlockSpec((2 * members, members), lambda i: (0, 0))],
        out_specs=block,
        compiler_params=pltpu.CompilerParams(vmem_limit_bytes=VMEM_LIMIT),
    )(forecast, folded)


def solution(mesh):
    cells = P(("grp", "gx"), "gy", "gz")
    in_specs = (
        P(("grp", "gx"), "gy", "gz", None),
        P(None, ("grp", "gx"), "gy", "gz"),
        cells,
        cells,
        cells,
        cells,
    )
    out_specs = P(("grp", "gx"), "gy", "gz", None)
    return jax.shard_map(
        per_device, mesh=mesh, in_specs=in_specs, out_specs=out_specs, check_vma=False
    )
```
